256 devices in a mesh: ctx: 32 (over y, x, core), ch: 8 (over z).
Axes of the slice: x: 4, y: 4, z: 8, core: 2. Of those that a mesh axis runs over, the one named last changes fastest.
Arguments:
- queries: bfloat16 [16384, 128], P('ctx'), may hold values from -6 to 6
- codes: int32 [16384], P('ctx'), may hold values from 0 to 511
- codebook: bfloat16 [512, 128], replicated, may hold values from -6 to 6
- values: bfloat16 [16384, 4096], P('ctx', 'ch'), may hold values from -6 to 6
- grad_out: bfloat16 [16384, 4096], P('ctx', 'ch'), may hold values from -0.75 to 0.75
- attn_out: bfloat16 [16384, 4096], P('ctx', 'ch'), may hold values from -6 to 6
- normalizer: float32 [16384], P('ctx'), as said below
Outputs:
- grad_values: bfloat16 [16384, 4096], P('ctx', 'ch')
- grad_queries: float32 [16384, 128], P('ctx')
- grad_codebook: float32 [512, 128], replicated
The draws below stay inside these ranges and needn't reach their ends.
Inputs may be any that keep to these rules, and one draw needn't show every extreme that they name: normalizer[t] lies within 0.3 of 0.5 ln(1 + t); it is used as given and is not recomputed from the scores.
All inputs are finite; a program needn't handle non-finite values.
Results may differ from the reference program's by a relative error of at most 0.0057.
Values sent between devices are 32-bit elements; how exact they have to be, the bound alone decides.
A program may use at most 192 MiB of HBM per device.

```python
import jax
import jax.numpy as jnp
from jax import lax

DK = 128
DV = 4096
CODES = 512
BLOCK = 512
TOKENS = 16384


def draw_normalizer(key, part):
    key = jax.random.fold_in(key, 7)
    position = jnp.arange(TOKENS, dtype=jnp.float32)
    noise = jax.random.uniform(key, (TOKENS,), jnp.float32, -0.3, 0.3)
    noise = jnp.where(position == 0.0, -0.3, noise)
    return 0.5 * jnp.log1p(position) + noise


def with_ends(values, stream_key, low, largest):
    dims = values.shape
    spot = [jax.random.randint(jax.random.fold_in(stream_key, axis), (), 0, dims[axis]) for axis in range(len(dims))]
    values = values.at[tuple(spot)].set(low)
    longest = dims.index(max(dims))
    spot[longest] = (spot[longest] + 1) % dims[longest]
    return values.at[tuple(spot)].set(largest)


def shard_levels(rng, extent, cuts, least, top_value):
    def one(dim, blocks):
        heights = jax.random.uniform(jax.random.fold_in(jax.random.fold_in(rng, 6), dim), (blocks,), jnp.float32, least / len(cuts), top_value / len(cuts))
        return jnp.repeat(jnp.exp(heights), extent[dim] // blocks).reshape((-1,) + (1,) * (len(extent) - dim - 1))

    factor_of = one(*cuts[0])
    for cut in cuts[1:]:
        factor_of = factor_of * one(*cut)
    return factor_of


def centred(stream_key, dims, scale, bound, split=(), kind=jnp.bfloat16):
    drawn = jax.random.normal(stream_key, dims, jnp.float32) * scale
    if len(split) > 0:
        drawn = shard_levels(stream_key, dims, split, -0.22, 0.18) * drawn
    return jnp.clip(drawn, min=-bound, max=bound).astype(kind)


def setup_inputs(seed: int = 0) -> dict:
    seeds = jax.random.split(jax.random.key(seed), 8)
    queries = centred(seeds[0], (TOKENS, DK), 1.0, 6.0, ((0, 32),))
    codes = with_ends(jax.random.randint(seeds[1], (TOKENS,), 0, CODES), jax.random.fold_in(seeds[1], 1), 0, CODES - 1).astype(jnp.int32)
    codebook = centred(seeds[2], (CODES, DK), 1.0, 6.0)
    values = centred(seeds[3], (TOKENS, DV), 1.0, 6.0, ((0, 32), (1, 8)))
    grad_out = centred(seeds[4], (TOKENS, DV), 0.125, 0.75, ((0, 32), (1, 8)))
    attn_out = centred(seeds[5], (TOKENS, DV), 1.0, 6.0, ((0, 32), (1, 8)))
    normalizer = draw_normalizer(jax.random.fold_in(seeds[7], 71), 0)
    return {"queries": queries, "codes": codes, "codebook": codebook, "values": values, "grad_out": grad_out, "attn_out": attn_out, "normalizer": normalizer}


def reference(queries, codes, codebook, values, grad_out, attn_out, normalizer):
    block_count = TOKENS // BLOCK
    score_scale = DK ** -0.5
    query_blocks = queries.reshape(block_count, BLOCK, DK)
    code_blocks = codes.reshape(block_count, BLOCK)
    value_blocks = values.reshape(block_count, BLOCK, DV)
    grad_blocks = grad_out.reshape(block_count, BLOCK, DV)
    out_blocks = attn_out.reshape(block_count, BLOCK, DV)
    norm_blocks = normalizer.reshape(block_count, BLOCK)
    code_ids = jnp.arange(CODES, dtype=jnp.int32)
    positions = jnp.arange(BLOCK, dtype=jnp.int32)
    causal = positions[:, None] >= positions[None, :]

    def code_weights(query, lognorm):
        logits = jnp.dot(query, codebook.T, preferred_element_type=jnp.float32) * score_scale
        return jnp.exp(logits - lognorm[:, None])

    def suffix_step(carried, inputs):
        query, code_row, grad, lognorm = inputs
        looked_up = jnp.take(carried, code_row, axis=0)
        weight_half = code_weights(query, lognorm).astype(jnp.bfloat16)
        carried = carried + jnp.dot(weight_half.T, grad, preferred_element_type=jnp.float32)
        return carried, looked_up

    _, lookups = lax.scan(suffix_step, jnp.zeros((CODES, DV), jnp.float32),
                          (query_blocks, code_blocks, grad_blocks, norm_blocks), reverse=True)

    def prefix_step(carried, inputs):
        total, count, grad_book = carried
        query, code_row, value, grad, output, lognorm, looked_up = inputs
        onehot = (code_row[:, None] == code_ids[None, :])
        keys = jnp.take(codebook, code_row, axis=0)
        logits = jnp.dot(query, keys.T, preferred_element_type=jnp.float32) * score_scale
        in_block = jnp.where(causal, jnp.exp(logits - lognorm[:, None]), 0.0)
        code_weight = code_weights(query, lognorm)
        row_delta = jnp.sum(grad.astype(jnp.float32) * output.astype(jnp.float32), axis=1)
        cross = jnp.dot(grad, value.T, preferred_element_type=jnp.float32)
        cached = jnp.dot(grad, total.astype(jnp.bfloat16).T, preferred_element_type=jnp.float32)
        dscore = in_block * (cross - row_delta[:, None])
        gathered = jnp.dot(dscore, onehot.astype(jnp.float32), precision=lax.Precision.HIGHEST)
        code_grad = (code_weight * (cached - count[None, :] * row_delta[:, None]) + gathered).astype(jnp.bfloat16)
        grad_query = jnp.dot(code_grad, codebook, preferred_element_type=jnp.float32) * score_scale
        grad_book = grad_book + jnp.dot(code_grad.T, query, preferred_element_type=jnp.float32) * score_scale
        grad_value = (jnp.dot(in_block.astype(jnp.bfloat16).T, grad, preferred_element_type=jnp.float32) + looked_up).astype(jnp.bfloat16)
        total = total + jnp.dot(onehot.astype(jnp.bfloat16).T, value, preferred_element_type=jnp.float32)
        count = count + jnp.sum(onehot.astype(jnp.float32), axis=0)
        return (total, count, grad_book), (grad_value, grad_query)

    start = (jnp.zeros((CODES, DV), jnp.float32), jnp.zeros((CODES,), jnp.float32), jnp.zeros((CODES, DK), jnp.float32))
    (_, _, grad_codebook), (grad_values, grad_queries) = lax.scan(
        prefix_step, start,
        (query_blocks, code_blocks, value_blocks, grad_blocks, out_blocks, norm_blocks, lookups))
    return grad_values.reshape(TOKENS, DV), grad_queries.reshape(TOKENS, DK), grad_codebook
```

```python
import functools

import jax
import jax.numpy as jnp
from jax import lax
from jax.experimental import pallas as pl
from jax.experimental.pallas import tpu as pltpu
from jax.sharding import PartitionSpec as P

MESH = pl.DeviceIdType.MESH
F32 = jnp.float32
BF16 = jnp.bfloat16

NN = (((1,), (0,)), ((), ()))
NT = (((1,), (1,)), ((), ()))


def dot(a, b, dims=NN):
    return lax.dot_general(a, b, dims, preferred_element_type=F32)


def split(x):
    high = x.astype(BF16)
    return high, (x - high.astype(F32)).astype(BF16)


def kernel(
    chips,
    depth,
    codes_ref,
    norm_ref,
    query_ref,
    book_ref,
    value_ref,
    grad_ref,
    out_ref,
    gv_ref,
    gq_ref,
    gb_ref,
    onehot,
    weight,
    probs,
    inner,
    local_values,
    sums,
    sums_x,
    sums_t,
    sums_in,
    sums_out,
    sums_p,
    sums_f,
    sums_h,
    grads,
    grads_x,
    grads_t,
    grads_in,
    grads_out,
    grads_p,
    grads_f,
    grads_h,
    tally,
    tally_x,
    tally_t,
    tally_in,
    book_p,
    book_x,
    book_t,
    book_in,
    book_s,
    book_z,
    book_o,
    book_r,
    book_h,
    gq_p,
    gq_in,
    gq_s,
    gq_r,
    core_send,
    core_recv,
    plane_send,
    plane_recv,
    z_send,
    z_recv,
):
    tokens, channels = value_ref.shape
    codes, dk = book_ref.shape
    half = codes // 2
    piece = half // chips
    zrows = dk // depth
    scale = float(dk) ** -0.5

    ctx = lax.axis_index("ctx")
    z = lax.axis_index("ch")
    chip = ctx // 2
    core = lax.rem(ctx, 2)
    other = chip * 2 + (1 - core)
    is_one = core.astype(F32)
    is_zero = 1.0 - is_one
    mine = pl.ds(pl.multiple_of(core * half, half), half)
    theirs = pl.ds(pl.multiple_of((1 - core) * half, half), half)

    def rows(k, size):
        return pl.ds(pl.multiple_of(k * size, size), size)

    def core_copy(n, src, dst):
        return pltpu.make_async_remote_copy(
            src_ref=src,
            dst_ref=dst,
            send_sem=core_send.at[n],
            recv_sem=core_recv.at[n],
            device_id={"ctx": other},
            device_id_type=MESH,
        )

    def plane_copy(n, k, src, dst, slot):
        return pltpu.make_async_remote_copy(
            src_ref=src,
            dst_ref=dst,
            send_sem=plane_send.at[n, k],
            recv_sem=plane_recv.at[n, slot],
            device_id={"ctx": k * 2 + core},
            device_id_type=MESH,
        )

    def z_copy(n, k, src, dst, slot):
        return pltpu.make_async_remote_copy(
            src_ref=src,
            dst_ref=dst,
            send_sem=z_send.at[n, k],
            recv_sem=z_recv.at[n, slot],
            device_id={"ch": k},
            device_id_type=MESH,
        )

    def over_plane(body):
        def step(i, carry):
            body(lax.rem(chip + i, chips))
            return carry

        lax.fori_loop(1, chips, step, 0)

    def over_z(body):
        def step(i, carry):
            body(lax.rem(z + i, depth))
            return carry

        lax.fori_loop(1, depth, step, 0)

    barrier = pltpu.get_barrier_semaphore()
    pl.semaphore_signal(barrier, inc=1, device_id={"ctx": other}, device_id_type=MESH)
    over_plane(
        lambda k: pl.semaphore_signal(
            barrier, inc=1, device_id={"ctx": k * 2 + core}, device_id_type=MESH
        )
    )
    over_z(lambda k: pl.semaphore_signal(barrier, inc=1, device_id={"ch": k}, device_id_type=MESH))

    code_row = codes_ref[...]
    onehot[...] = jnp.where(
        lax.broadcasted_iota(jnp.int32, (codes, tokens), 0) == code_row, 1.0, 0.0
    ).astype(BF16)
    sums[...] = dot(onehot[...], value_ref[...])
    tally[...] = dot(jnp.ones((8, tokens), BF16), onehot[...], NT)

    pl.semaphore_wait(barrier, 1 + (chips - 1) + (depth - 1))

    s_core = core_copy(0, sums.at[theirs], sums_x)
    s_core.start()
    t_core = core_copy(1, tally, tally_x)
    t_core.start()

    norm_row = norm_ref[...]
    weight[...] = jnp.exp(dot(book_ref[...], query_ref[...], NT) * scale - norm_row)
    grads[...] = dot(weight[...].astype(BF16), grad_ref[...])
    g_core = core_copy(2, grads.at[theirs], grads_x)
    g_core.start()

    s_core.wait_recv()
    sums_t[...] = sums[mine] + sums_x[...]
    over_plane(
        lambda k: plane_copy(0, k, sums_t.at[rows(k, piece)], sums_in.at[chip], chip).start()
    )
    sums_in[chip] = sums_t[rows(chip, piece)]
    t_core.wait_recv()
    tally_t[...] = tally[...] + tally_x[...]
    over_plane(lambda k: plane_copy(1, k, tally_t, tally_in.at[chip], chip).start())
    tally_in[chip] = tally_t[...]

    g_core.wait_recv()
    grads_t[...] = grads[mine] + grads_x[...]
    over_plane(
        lambda k: plane_copy(2, k, grads_t.at[rows(k, piece)], grads_in.at[chip], chip).start()
    )
    grads_in[chip] = grads_t[rows(chip, piece)]

    key_t = dot(book_ref[...].astype(F32).T.astype(BF16), onehot[...]).astype(BF16)
    keys = key_t.astype(F32).T.astype(BF16)
    causal = lax.broadcasted_iota(jnp.int32, (tokens, tokens), 0) <= lax.broadcasted_iota(
        jnp.int32, (tokens, tokens), 1
    )
    in_block = jnp.where(
        causal, jnp.exp(dot(keys, query_ref[...], NT) * scale - norm_row), 0.0
    )
    probs[...] = in_block.astype(BF16)
    product = grad_ref[...].astype(F32) * out_ref[...].astype(F32)
    product_high, product_low = split(product)
    ones = jnp.ones((8, channels), BF16)
    delta = (dot(ones, product_high, NT) + dot(ones, product_low, NT))[0:1]
    dscore = in_block * (dot(value_ref[...], grad_ref[...], NT) - delta)
    dscore_high, dscore_low = split(dscore)
    inner[...] = dot(onehot[...], dscore_high) + dot(onehot[...], dscore_low)

    def wait_plane(n, buffer):
        over_plane(lambda k: plane_copy(n, k, buffer.at[k], buffer.at[k], k).wait_recv())

    def scan(buffer, result, backward):
        def step(i, total):
            k = chips - 1 - i if backward else i
            result[k] = total
            return total + buffer[k]

        lax.fori_loop(0, chips, step, jnp.zeros((piece, channels), F32))

    wait_plane(0, sums_in)
    scan(sums_in, sums_out, False)
    over_plane(
        lambda k: plane_copy(3, k, sums_out.at[k], sums_p.at[rows(chip, piece)], chip).start()
    )
    sums_p[rows(chip, piece)] = sums_out[chip]
    wait_plane(2, grads_in)
    scan(grads_in, grads_out, True)
    over_plane(
        lambda k: plane_copy(4, k, grads_out.at[k], grads_p.at[rows(chip, piece)], chip).start()
    )
    grads_p[rows(chip, piece)] = grads_out[chip]

    local_values[...] = dot(probs[...], grad_ref[...])

    wait_plane(1, tally_in)

    def count_step(k, total):
        return total + jnp.where(k < chip, 1.0, 0.0) * tally_in[k]

    count = lax.fori_loop(0, chips, count_step, is_one * tally_x[...])
    count_col = jnp.broadcast_to(count[0:1], (128, codes)).T[:, 0:1]

    def wait_rows(n, buffer, size):
        over_plane(
            lambda k: plane_copy(
                n, k, buffer.at[rows(k, size)], buffer.at[rows(k, size)], k
            ).wait_recv()
        )

    wait_rows(3, sums_p, piece)
    sums_f[...] = sums_p[...] + is_zero * sums[mine]
    s_back = core_copy(3, sums_f, sums_h)
    s_back.start()
    own_half = (sums_p[...] + is_one * sums_x[...]).astype(BF16)
    cached_own = dot(own_half, grad_ref[...], NT)
    cgrad_own = (
        weight[mine] * (cached_own - jnp.where(core == 1, count_col[half:], count_col[:half]) * delta)
        + inner[mine]
    )
    s_back.wait_recv()
    cached_other = dot(sums_h[...].astype(BF16), grad_ref[...], NT)
    cgrad_other = (
        weight[theirs]
        * (cached_other - jnp.where(core == 1, count_col[:half], count_col[half:]) * delta)
        + inner[theirs]
    )
    own_high, own_low = split(cgrad_own)
    other_high, other_low = split(cgrad_other)
    query = query_ref[...]
    book_p[0] = (dot(own_high, query) + dot(own_low, query)) * scale
    book_p[1] = (dot(other_high, query) + dot(other_low, query)) * scale
    b_core = core_copy(5, book_p.at[1], book_x)
    b_core.start()
    book_own = book_ref[mine].astype(F32).T.astype(BF16)
    book_other = book_ref[theirs].astype(F32).T.astype(BF16)
    gq_p[...] = (
        dot(book_own, own_high)
        + dot(book_own, own_low)
        + dot(book_other, other_high)
        + dot(book_other, other_low)
    ) * scale
    over_z(lambda k: z_copy(0, k, gq_p.at[rows(k, zrows)], gq_in.at[z], z).start())
    gq_in[z] = gq_p[rows(z, zrows)]

    b_core.wait_recv()
    book_t[...] = book_p[0] + book_x[...]
    over_plane(lambda k: plane_copy(5, k, book_t.at[rows(k, piece)], book_in.at[chip], chip).start())
    book_in[chip] = book_t[rows(chip, piece)]

    wait_rows(4, grads_p, piece)
    grads_f[...] = grads_p[...] + is_one * grads[mine]
    g_back = core_copy(4, grads_f, grads_h)
    g_back.start()

    wait_plane(5, book_in)
    book_s[...] = lax.fori_loop(
        0, chips, lambda k, total: total + book_in[k], jnp.zeros((piece, dk), F32)
    )
    over_z(lambda k: z_copy(1, k, book_s, book_z.at[z], z).start())
    book_z[z] = book_s[...]

    def wait_z(n, buffer):
        over_z(lambda k: z_copy(n, k, buffer.at[k], buffer.at[k], k).wait_recv())

    wait_z(0, gq_in)
    gq_s[...] = lax.fori_loop(
        0, depth, lambda k, total: total + gq_in[k], jnp.zeros((zrows, tokens), F32)
    )
    over_z(lambda k: z_copy(2, k, gq_s, gq_r.at[rows(z, zrows)], z).start())
    gq_r[rows(z, zrows)] = gq_s[...]

    wait_z(1, book_z)
    book_o[...] = lax.fori_loop(
        0, depth, lambda k, total: total + book_z[k], jnp.zeros((piece, dk), F32)
    )
    over_plane(lambda k: plane_copy(6, k, book_o, book_r.at[rows(chip, piece)], chip).start())
    book_r[rows(chip, piece)] = book_o[...]

    own_later = grads_p[...] + is_zero * grads_x[...]
    lookup = onehot[...].T
    low_half = core == 0
    g_back.wait_recv()
    other_later = grads_h[...]
    first = jnp.where(low_half, own_later, other_later)
    second = jnp.where(low_half, other_later, own_later)
    first_high, first_low = split(first)
    second_high, second_low = split(second)
    looked_up = (
        dot(lookup[:, :half], first_high)
        + dot(lookup[:, :half], first_low)
        + dot(lookup[:, half:], second_high)
        + dot(lookup[:, half:], second_low)
    )
    gv_ref[...] = (local_values[...] + looked_up).astype(BF16)

    wait_rows(6, book_r, piece)
    b_back = core_copy(6, book_r, book_h)
    b_back.start()
    over_z(
        lambda k: z_copy(2, k, gq_r.at[rows(k, zrows)], gq_r.at[rows(k, zrows)], k).wait_recv()
    )
    gq_ref[...] = gq_r[...].T
    gb_ref[mine] = book_r[...]
    b_back.wait_recv()
    gb_ref[theirs] = book_h[...]

    for copy in (s_core, t_core, g_core, s_back, b_core, g_back, b_back):
        copy.wait_send()

    def drain_plane(k):
        plane_copy(0, k, sums_t.at[rows(k, piece)], sums_in.at[chip], chip).wait_send()
        plane_copy(1, k, tally_t, tally_in.at[chip], chip).wait_send()
        plane_copy(2, k, grads_t.at[rows(k, piece)], grads_in.at[chip], chip).wait_send()
        plane_copy(3, k, sums_out.at[k], sums_p.at[rows(chip, piece)], chip).wait_send()
        plane_copy(4, k, grads_out.at[k], grads_p.at[rows(chip, piece)], chip).wait_send()
        plane_copy(5, k, book_t.at[rows(k, piece)], book_in.at[chip], chip).wait_send()
        plane_copy(6, k, book_o, book_r.at[rows(chip, piece)], chip).wait_send()

    def drain_z(k):
        z_copy(0, k, gq_p.at[rows(k, zrows)], gq_in.at[z], z).wait_send()
        z_copy(1, k, book_s, book_z.at[z], z).wait_send()
        z_copy(2, k, gq_s, gq_r.at[rows(z, zrows)], z).wait_send()

    over_plane(drain_plane)
    over_z(drain_z)


def local(chips, depth, queries, codes, codebook, values, grad_out, attn_out, normalizer):
    tokens, channels = values.shape
    count, dk = codebook.shape
    half = count // 2
    piece = half // chips
    zrows = dk // depth

    def f32(*shape):
        return pltpu.VMEM(shape, F32)

    def scan_scratch():
        return [
            f32(count, channels),
            f32(half, channels),
            f32(half, channels),
            f32(chips, piece, channels),
            f32(chips, piece, channels),
            f32(half, channels),
            f32(half, channels),
            f32(half, channels),
        ]

    scratch = (
        [
            pltpu.VMEM((count, tokens), BF16),
            f32(count, tokens),
            pltpu.VMEM((tokens, tokens), BF16),
            f32(count, tokens),
            f32(tokens, channels),
        ]
        + scan_scratch()
        + scan_scratch()
        + [f32(8, count), f32(8, count), f32(8, count), f32(chips, 8, count)]
        + [
            f32(2, half, dk),
            f32(half, dk),
            f32(half, dk),
            f32(chips, piece, dk),
            f32(piece, dk),
            f32(depth, piece, dk),
            f32(piece, dk),
            f32(half, dk),
            f32(half, dk),
        ]
        + [f32(dk, tokens), f32(depth, zrows, tokens), f32(zrows, tokens), f32(dk, tokens)]
        + [
            pltpu.SemaphoreType.DMA((7,)),
            pltpu.SemaphoreType.DMA((7,)),
            pltpu.SemaphoreType.DMA((7, chips)),
            pltpu.SemaphoreType.DMA((7, chips)),
            pltpu.SemaphoreType.DMA((3, depth)),
            pltpu.SemaphoreType.DMA((3, depth)),
        ]
    )
    return pl.pallas_call(
        functools.partial(kernel, chips, depth),
        out_shape=(
            jax.ShapeDtypeStruct((tokens, channels), BF16),
            jax.ShapeDtypeStruct((tokens, dk), F32),
            jax.ShapeDtypeStruct((count, dk), F32),
        ),
        in_specs=[pl.BlockSpec(memory_space=pltpu.VMEM)] * 7,
        out_specs=[pl.BlockSpec(memory_space=pltpu.VMEM)] * 3,
        scratch_shapes=scratch,
        compiler_params=pltpu.CompilerParams(
            collective_id=0, has_side_effects=True, vmem_limit_bytes=56 * 1024 * 1024
        ),
        name="vq_backward",
    )(
        codes.reshape(1, tokens),
        normalizer.reshape(1, tokens),
        queries,
        codebook,
        values,
        grad_out,
        attn_out,
    )


def solution(mesh):
    in_specs = (
        P("ctx", None),
        P("ctx"),
        P(),
        P("ctx", "ch"),
        P("ctx", "ch"),
        P("ctx", "ch"),
        P("ctx"),
    )
    out_specs = (P("ctx", "ch"), P("ctx", None), P())
    step = functools.partial(local, mesh.shape["ctx"] // 2, mesh.shape["ch"])
    return jax.shard_map(step, mesh=mesh, in_specs=in_specs, out_specs=out_specs, check_vma=False)
```

```python
import functools

import jax
import jax.numpy as jnp
from jax import lax
from jax.experimental import pallas as pl
from jax.experimental.pallas import tpu as pltpu
from jax.sharding import PartitionSpec as P

MESH = pl.DeviceIdType.MESH
EARLY = 8
F32 = jnp.float32
BF16 = jnp.bfloat16

FAR_FIRST = (
    ((2, 2), (2, 1), (1, 2), (2, 3), (3, 2), (1, 1), (1, 3), (3, 1), (3, 3), (2, 0), (0, 2))
    + ((1, 0), (3, 0), (0, 1), (0, 3))
)

NN = (((1,), (0,)), ((), ()))
NT = (((1,), (1,)), ((), ()))


def dot(a, b, dims=NN):
    return lax.dot_general(a, b, dims, preferred_element_type=F32)


def split(x):
    high = x.astype(BF16)
    return high, (x - high.astype(F32)).astype(BF16)


def kernel(
    chips,
    depth,
    codes_hbm,
    value_hbm,
    book_hbm,
    query_hbm,
    norm_hbm,
    grad_hbm,
    out_hbm,
    gv_ref,
    gq_ref,
    gb_ref,
    codes_ref,
    value_ref,
    book_ref,
    query_ref,
    norm_ref,
    grad_ref,
    out_ref,
    load_sem,
    onehot,
    weight,
    probs,
    inner,
    local_values,
    sums,
    sums_x,
    sums_t,
    sums_in,
    sums_out,
    sums_p,
    sums_f,
    sums_h,
    grads,
    grads_x,
    grads_t,
    grads_in,
    grads_out,
    grads_p,
    grads_f,
    grads_h,
    tally,
    tally_x,
    tally_t,
    tally_in,
    book_p,
    book_x,
    book_t,
    book_in,
    book_s,
    book_z,
    book_o,
    book_r,
    book_h,
    gq_p,
    gq_in,
    gq_s,
    gq_r,
    core_send,
    core_recv,
    plane_send,
    plane_recv,
    z_send,
    z_recv,
):
    tokens, channels = value_ref.shape
    codes, dk = book_ref.shape
    half = codes // 2
    piece = half // chips
    zrows = dk // depth
    early = EARLY
    scale = float(dk) ** -0.5

    ctx = lax.axis_index("ctx")
    z = lax.axis_index("ch")
    chip = ctx // 2
    core = lax.rem(ctx, 2)
    other = chip * 2 + (1 - core)
    is_one = core.astype(F32)
    is_zero = 1.0 - is_one
    mine = pl.ds(pl.multiple_of(core * half, half), half)
    theirs = pl.ds(pl.multiple_of((1 - core) * half, half), half)

    def rows(k, size):
        return pl.ds(pl.multiple_of(k * size, size), size)

    def core_copy(n, src, dst):
        return pltpu.make_async_remote_copy(
            src_ref=src,
            dst_ref=dst,
            send_sem=core_send.at[n],
            recv_sem=core_recv.at[n],
            device_id={"ctx": other},
            device_id_type=MESH,
        )

    def plane_copy(n, k, src, dst):
        return pltpu.make_async_remote_copy(
            src_ref=src,
            dst_ref=dst,
            send_sem=plane_send.at[n],
            recv_sem=plane_recv.at[n],
            device_id={"ctx": k * 2 + core},
            device_id_type=MESH,
        )

    def z_copy(n, k, src, dst):
        return pltpu.make_async_remote_copy(
            src_ref=src,
            dst_ref=dst,
            send_sem=z_send.at[n],
            recv_sem=z_recv.at[n],
            device_id={"ch": k},
            device_id_type=MESH,
        )

    def over_plane(body):
        def step(i, carry):
            body(lax.rem(chip + i, chips))
            return carry

        lax.fori_loop(1, chips, step, 0)

    def far_first(body):
        y, x = chip // 4, lax.rem(chip, 4)
        for dy, dx in FAR_FIRST:
            body(lax.rem(y + dy, 4) * 4 + lax.rem(x + dx, 4))

    def over_z(body):
        def step(i, carry):
            body(lax.rem(z + i, depth))
            return carry

        lax.fori_loop(1, depth, step, 0)

    loads = [
        pltpu.make_async_copy(source, target, load_sem.at[n])
        for n, (source, target) in enumerate(
            (
                (codes_hbm, codes_ref),
                (value_hbm, value_ref),
                (book_hbm, book_ref),
                (query_hbm, query_ref),
                (norm_hbm, norm_ref),
                (grad_hbm, grad_ref),
                (out_hbm, out_ref),
            )
        )
    ]
    for load in loads:
        load.start()

    barrier = pltpu.get_barrier_semaphore()
    pl.semaphore_signal(barrier, inc=1, device_id={"ctx": other}, device_id_type=MESH)
    over_plane(
        lambda k: pl.semaphore_signal(
            barrier, inc=1, device_id={"ctx": k * 2 + core}, device_id_type=MESH
        )
    )
    over_z(lambda k: pl.semaphore_signal(barrier, inc=1, device_id={"ch": k}, device_id_type=MESH))

    loads[0].wait()
    code_row = codes_ref[...]
    onehot[...] = jnp.where(
        lax.broadcasted_iota(jnp.int32, (codes, tokens), 0) == code_row, 1.0, 0.0
    ).astype(BF16)
    loads[1].wait()
    sums[...] = dot(onehot[...], value_ref[...])
    tally[...] = dot(jnp.ones((8, tokens), BF16), onehot[...], NT)[0:1]

    pl.semaphore_wait(barrier, 1 + (chips - 1) + (depth - 1))

    s_core = core_copy(0, sums.at[theirs], sums_x)
    s_core.start()
    t_core = core_copy(1, tally, tally_x)
    t_core.start()

    for load in loads[2:]:
        load.wait()
    norm_row = norm_ref[...]
    weight[...] = jnp.exp(dot(book_ref[...], query_ref[...], NT) * scale - norm_row)
    grads[...] = dot(weight[...].astype(BF16), grad_ref[...])
    g_core = core_copy(2, grads.at[theirs], grads_x)
    g_core.start()

    s_core.wait_recv()
    sums_t[...] = sums[mine] + sums_x[...]
    far_first(lambda k: plane_copy(0, k, sums_t.at[rows(k, piece)], sums_in.at[chip]).start())
    sums_in[chip] = sums_t[rows(chip, piece)]

    g_core.wait_recv()
    grads_t[...] = grads[mine] + grads_x[...]
    grads_in[chip] = grads_t[rows(chip, piece)]

    def grads_part(n, first, size):
        def send(k):
            source = grads_t.at[pl.ds(pl.multiple_of(k * piece + first, 8), size)]
            plane_copy(n, k, source, grads_in.at[chip, pl.ds(first, size)]).start()

        over_plane(send)

    if early:
        grads_part(2, 0, early)

    t_core.wait_recv()
    tally_t[...] = tally[...] + tally_x[...]
    over_plane(lambda k: plane_copy(1, k, tally_t, tally_in.at[chip]).start())
    tally_in[chip] = tally_t[...]

    key_t = dot(book_ref[...].astype(F32).T.astype(BF16), onehot[...]).astype(BF16)
    keys = key_t.astype(F32).T.astype(BF16)
    causal = lax.broadcasted_iota(jnp.int32, (tokens, tokens), 0) <= lax.broadcasted_iota(
        jnp.int32, (tokens, tokens), 1
    )
    in_block = jnp.where(
        causal, jnp.exp(dot(keys, query_ref[...], NT) * scale - norm_row), 0.0
    )
    probs[...] = in_block.astype(BF16)
    product = grad_ref[...].astype(F32) * out_ref[...].astype(F32)
    product_high, product_low = split(product)
    ones = jnp.ones((8, channels), BF16)
    delta = (dot(ones, product_high, NT) + dot(ones, product_low, NT))[0:1]
    dscore = in_block * (dot(value_ref[...], grad_ref[...], NT) - delta)
    dscore_high, dscore_low = split(dscore)
    inner[...] = dot(onehot[...], dscore_high) + dot(onehot[...], dscore_low)

    def plane_bytes(n, ref):
        return plane_copy(n, chip, ref, ref)

    def z_bytes(n, ref):
        return z_copy(n, z, ref, ref)

    def wait_plane(n, buffer):
        plane_bytes(n, buffer.at[pl.ds(0, chips - 1)]).wait_recv()

    def scan(buffer, result, backward):
        def step(i, total):
            k = chips - 1 - i if backward else i
            result[k] = total
            return total + buffer[k]

        lax.fori_loop(0, chips, step, jnp.zeros((piece, channels), F32))

    early_bytes = grads_t.at[pl.ds(0, (chips - 1) * early)]
    late_bytes = grads_t.at[pl.ds(0, (chips - 1) * (piece - early))]
    wait_plane(0, sums_in)
    scan(sums_in, sums_out, False)
    far_first(
        lambda k: plane_copy(3, k, sums_out.at[k], sums_p.at[rows(chip, piece)]).start()
    )
    sums_p[rows(chip, piece)] = sums_out[chip]
    local_values[...] = dot(probs[...], grad_ref[...])

    wait_plane(1, tally_in)

    def count_step(k, total):
        return total + jnp.where(k < chip, 1.0, 0.0) * tally_in[k]

    count = lax.fori_loop(0, chips, count_step, is_one * tally_x[...])
    count_col = jnp.broadcast_to(count, (128, codes)).T[:, 0:1]

    def wait_rows(n, buffer, size):
        plane_bytes(n, buffer.at[pl.ds(0, (chips - 1) * size)]).wait_recv()

    wait_rows(3, sums_p, piece)
    sums_f[...] = sums_p[...] + is_zero * sums[mine]
    s_back = core_copy(3, sums_f, sums_h)
    s_back.start()
    if early < piece:
        grads_part(7, early, piece - early)
    query = query_ref[...]

    def code_grad(cache, span, counts):
        cached = dot(cache, grad_ref[...], NT)
        return split(weight[span] * (cached - counts * delta) + inner[span])

    low_counts, high_counts = count_col[:half], count_col[half:]
    high, low = code_grad(
        (sums_p[...] + is_one * sums_x[...]).astype(BF16),
        mine,
        jnp.where(core == 1, high_counts, low_counts),
    )
    book_p[0] = (dot(high, query) + dot(low, query)) * scale
    book_part = book_ref[mine].astype(F32).T.astype(BF16)
    gq_p[...] = dot(book_part, high) + dot(book_part, low)
    book_part = book_ref[theirs].astype(F32).T.astype(BF16)
    s_back.wait_recv()
    high, low = code_grad(
        sums_h[...].astype(BF16), theirs, jnp.where(core == 1, low_counts, high_counts)
    )
    book_p[1] = (dot(high, query) + dot(low, query)) * scale
    b_core = core_copy(5, book_p.at[1], book_x)
    b_core.start()
    gq_p[...] = (gq_p[...] + dot(book_part, high) + dot(book_part, low)) * scale
    over_z(lambda k: z_copy(0, k, gq_p.at[rows(k, zrows)], gq_in.at[z]).start())
    gq_in[z] = gq_p[rows(z, zrows)]

    b_core.wait_recv()
    book_t[...] = book_p[0] + book_x[...]
    over_plane(lambda k: plane_copy(5, k, book_t.at[rows(k, piece)], book_in.at[chip]).start())
    book_in[chip] = book_t[rows(chip, piece)]

    if early:
        plane_bytes(2, early_bytes).wait_recv()
    if early < piece:
        plane_bytes(7, late_bytes).wait_recv()
    scan(grads_in, grads_out, True)
    over_plane(
        lambda k: plane_copy(4, k, grads_out.at[k], grads_p.at[rows(chip, piece)]).start()
    )
    grads_p[rows(chip, piece)] = grads_out[chip]

    wait_plane(5, book_in)
    book_s[...] = lax.fori_loop(
        0, chips, lambda k, total: total + book_in[k], jnp.zeros((piece, dk), F32)
    )
    over_z(lambda k: z_copy(1, k, book_s, book_z.at[z]).start())
    book_z[z] = book_s[...]

    def wait_z(n, buffer):
        z_bytes(n, buffer.at[pl.ds(0, depth - 1)]).wait_recv()

    wait_z(0, gq_in)
    gq_s[...] = lax.fori_loop(
        0, depth, lambda k, total: total + gq_in[k], jnp.zeros((zrows, tokens), F32)
    )
    over_z(lambda k: z_copy(2, k, gq_s, gq_r.at[rows(z, zrows)]).start())
    gq_r[rows(z, zrows)] = gq_s[...]

    wait_z(1, book_z)
    book_o[...] = lax.fori_loop(
        0, depth, lambda k, total: total + book_z[k], jnp.zeros((piece, dk), F32)
    )
    over_plane(lambda k: plane_copy(6, k, book_o, book_r.at[rows(chip, piece)]).start())
    book_r[rows(chip, piece)] = book_o[...]

    wait_rows(4, grads_p, piece)
    grads_f[...] = grads_p[...] + is_one * grads[mine]
    g_back = core_copy(4, grads_f, grads_h)
    g_back.start()

    own_later = grads_p[...] + is_zero * grads_x[...]
    lookup = onehot[...].T
    low_half = core == 0
    g_back.wait_recv()
    other_later = grads_h[...]
    first = jnp.where(low_half, own_later, other_later)
    second = jnp.where(low_half, other_later, own_later)
    first_high, first_low = split(first)
    second_high, second_low = split(second)
    looked_up = (
        dot(lookup[:, :half], first_high)
        + dot(lookup[:, :half], first_low)
        + dot(lookup[:, half:], second_high)
        + dot(lookup[:, half:], second_low)
    )
    gv_ref[...] = (local_values[...] + looked_up).astype(BF16)

    wait_rows(6, book_r, piece)
    b_back = core_copy(6, book_r, book_h)
    b_back.start()
    z_bytes(2, gq_r.at[pl.ds(0, (depth - 1) * zrows)]).wait_recv()
    gq_ref[...] = gq_r[...].T
    gb_ref[mine] = book_r[...]
    b_back.wait_recv()
    gb_ref[theirs] = book_h[...]

    for copy in (s_core, t_core, g_core, s_back, b_core, g_back, b_back):
        copy.wait_send()

    for n, ref in ((0, sums_in), (1, tally_in), (3, sums_out), (4, grads_out), (5, book_in)):
        plane_bytes(n, ref.at[pl.ds(0, chips - 1)]).wait_send()
    if early:
        plane_bytes(2, early_bytes).wait_send()
    if early < piece:
        plane_bytes(7, late_bytes).wait_send()
    plane_bytes(6, book_r.at[pl.ds(0, (chips - 1) * piece)]).wait_send()
    z_bytes(0, gq_in.at[pl.ds(0, depth - 1)]).wait_send()
    z_bytes(1, book_z.at[pl.ds(0, depth - 1)]).wait_send()
    z_bytes(2, gq_r.at[pl.ds(0, (depth - 1) * zrows)]).wait_send()


def store(gv_ref, gq_ref, gb_ref, gv_hbm, gq_hbm, gb_hbm, sem):
    copies = [
        pltpu.make_async_copy(source, target, sem.at[n])
        for n, (source, target) in enumerate(
            ((gv_ref, gv_hbm), (gq_ref, gq_hbm), (gb_ref, gb_hbm))
        )
    ]
    for copy in copies:
        copy.start()
    for copy in copies:
        copy.wait()


def local(chips, depth, queries, codes, codebook, values, grad_out, attn_out, normalizer):
    tokens, channels = values.shape
    count, dk = codebook.shape
    half = count // 2
    piece = half // chips
    zrows = dk // depth

    def f32(*shape):
        return pltpu.VMEM(shape, F32)

    def scan_scratch():
        return [
            f32(count, channels),
            f32(half, channels),
            f32(half, channels),
            f32(chips, piece, channels),
            f32(chips, piece, channels),
            f32(half, channels),
            f32(half, channels),
            f32(half, channels),
        ]

    scratch = (
        [
            pltpu.VMEM((1, tokens), jnp.int32),
            pltpu.VMEM((tokens, channels), BF16),
            pltpu.VMEM((count, dk), BF16),
            pltpu.VMEM((tokens, dk), BF16),
            f32(1, tokens),
            pltpu.VMEM((tokens, channels), BF16),
            pltpu.VMEM((tokens, channels), BF16),
            pltpu.SemaphoreType.DMA((7,)),
            pltpu.VMEM((count, tokens), BF16),
            f32(count, tokens),
            pltpu.VMEM((tokens, tokens), BF16),
            f32(count, tokens),
            f32(tokens, channels),
        ]
        + scan_scratch()
        + scan_scratch()
        + [f32(1, count), f32(1, count), f32(1, count), f32(chips, 1, count)]
        + [
            f32(2, half, dk),
            f32(half, dk),
            f32(half, dk),
            f32(chips, piece, dk),
            f32(piece, dk),
            f32(depth, piece, dk),
            f32(piece, dk),
            f32(half, dk),
            f32(half, dk),
        ]
        + [f32(dk, tokens), f32(depth, zrows, tokens), f32(zrows, tokens), f32(dk, tokens)]
        + [
            pltpu.SemaphoreType.DMA((8,)),
            pltpu.SemaphoreType.DMA((8,)),
            pltpu.SemaphoreType.DMA((8,)),
            pltpu.SemaphoreType.DMA((8,)),
            pltpu.SemaphoreType.DMA((3,)),
            pltpu.SemaphoreType.DMA((3,)),
        ]
    )
    results = pl.pallas_call(
        functools.partial(kernel, chips, depth),
        out_shape=(
            pltpu.VMEM((tokens, channels), BF16),
            pltpu.VMEM((tokens, dk), F32),
            pltpu.VMEM((count, dk), F32),
        ),
        in_specs=[pl.BlockSpec(memory_space=pltpu.HBM)] * 7,
        out_specs=[pl.BlockSpec(memory_space=pltpu.VMEM)] * 3,
        scratch_shapes=scratch,
        compiler_params=pltpu.CompilerParams(
            collective_id=0, has_side_effects=True, vmem_limit_bytes=60 * 1024 * 1024
        ),
        name="vq_backward",
    )(
        codes.reshape(1, tokens),
        values,
        codebook,
        queries,
        normalizer.reshape(1, tokens),
        grad_out,
        attn_out,
    )
    return pl.pallas_call(
        store,
        out_shape=(
            jax.ShapeDtypeStruct((tokens, channels), BF16),
            jax.ShapeDtypeStruct((tokens, dk), F32),
            jax.ShapeDtypeStruct((count, dk), F32),
        ),
        in_specs=[pl.BlockSpec(memory_space=pl.ANY)] * 3,
        out_specs=[pl.BlockSpec(memory_space=pltpu.HBM)] * 3,
        scratch_shapes=[pltpu.SemaphoreType.DMA((3,))],
        compiler_params=pltpu.CompilerParams(vmem_limit_bytes=4 * 1024 * 1024),
        name="store",
    )(*results)


def solution(mesh):
    in_specs = (
        P("ctx", None),
        P("ctx"),
        P(),
        P("ctx", "ch"),
        P("ctx", "ch"),
        P("ctx", "ch"),
        P("ctx"),
    )
    out_specs = (P("ctx", "ch"), P("ctx", None), P())
    step = functools.partial(local, mesh.shape["ctx"] // 2, mesh.shape["ch"])
    return jax.shard_map(step, mesh=mesh, in_specs=in_specs, out_specs=out_specs, check_vma=False)
```

```python
import functools

import jax
import jax.numpy as jnp
from jax import lax
from jax.experimental import pallas as pl
from jax.experimental.pallas import tpu as pltpu
from jax.sharding import PartitionSpec as P

MESH = pl.DeviceIdType.MESH
EARLY = 8
F32 = jnp.float32
BF16 = jnp.bfloat16

FAR_FIRST = (
    ((2, 2), (2, 1), (1, 2), (2, 3), (3, 2), (1, 1), (1, 3), (3, 1), (3, 3), (2, 0), (0, 2))
    + ((1, 0), (3, 0), (0, 1), (0, 3))
)

NN = (((1,), (0,)), ((), ()))
NT = (((1,), (1,)), ((), ()))


def dot(a, b, dims=NN):
    return lax.dot_general(a, b, dims, preferred_element_type=F32)


def split(x):
    high = x.astype(BF16)
    return high, (x - high.astype(F32)).astype(BF16)


def kernel(
    chips,
    depth,
    codes_hbm,
    value_hbm,
    book_hbm,
    query_hbm,
    norm_hbm,
    grad_hbm,
    out_hbm,
    gv_ref,
    gq_ref,
    gb_ref,
    codes_ref,
    value_ref,
    book_ref,
    query_ref,
    norm_ref,
    grad_ref,
    out_ref,
    load_sem,
    onehot,
    weight,
    probs,
    inner,
    local_values,
    sums,
    sums_x,
    sums_t,
    sums_in,
    sums_out,
    sums_p,
    grads,
    grads_x,
    grads_t,
    grads_in,
    grads_out,
    grads_p,
    grads_f,
    grads_h,
    query_s,
    query_x,
    grad_s,
    grad_x,
    grad_o,
    weight_o,
    inner_x,
    norm_x,
    delta_s,
    delta_x,
    lookup,
    tally,
    tally_x,
    tally_t,
    tally_in,
    book_t,
    book_in,
    book_s,
    book_z,
    book_o,
    book_r,
    book_h,
    gq_o,
    gq_x,
    gq_p,
    gq_in,
    gq_s,
    gq_r,
    core_send,
    core_recv,
    plane_send,
    plane_recv,
    z_send,
    z_recv,
):
    tokens, channels = value_ref.shape
    codes, dk = book_ref.shape
    half = codes // 2
    piece = half // chips
    zrows = dk // depth
    early = EARLY
    scale = float(dk) ** -0.5

    ctx = lax.axis_index("ctx")
    z = lax.axis_index("ch")
    chip = ctx // 2
    core = lax.rem(ctx, 2)
    other = chip * 2 + (1 - core)
    is_one = core.astype(F32)
    is_zero = 1.0 - is_one
    mine = pl.ds(pl.multiple_of(core * half, half), half)
    theirs = pl.ds(pl.multiple_of((1 - core) * half, half), half)

    def rows(k, size):
        return pl.ds(pl.multiple_of(k * size, size), size)

    def core_copy(n, src, dst):
        return pltpu.make_async_remote_copy(
            src_ref=src,
            dst_ref=dst,
            send_sem=core_send.at[n],
            recv_sem=core_recv.at[n],
            device_id={"ctx": other},
            device_id_type=MESH,
        )

    def plane_copy(n, k, src, dst):
        return pltpu.make_async_remote_copy(
            src_ref=src,
            dst_ref=dst,
            send_sem=plane_send.at[n],
            recv_sem=plane_recv.at[n],
            device_id={"ctx": k * 2 + core},
            device_id_type=MESH,
        )

    def z_copy(n, k, src, dst):
        return pltpu.make_async_remote_copy(
            src_ref=src,
            dst_ref=dst,
            send_sem=z_send.at[n],
            recv_sem=z_recv.at[n],
            device_id={"ch": k},
            device_id_type=MESH,
        )

    def over_plane(body):
        def step(i, carry):
            body(lax.rem(chip + i, chips))
            return carry

        lax.fori_loop(1, chips, step, 0)

    def far_first(body):
        y, x = chip // 4, lax.rem(chip, 4)
        for dy, dx in FAR_FIRST:
            body(lax.rem(y + dy, 4) * 4 + lax.rem(x + dx, 4))

    def over_z(body):
        half_way = depth // 2
        body(lax.rem(z + half_way, depth))

        def step(i, carry):
            body(lax.rem(z + half_way + i, depth))
            body(lax.rem(z + half_way - i, depth))
            return carry

        lax.fori_loop(1, half_way, step, 0)

    loads = [
        pltpu.make_async_copy(source, target, load_sem.at[n])
        for n, (source, target) in enumerate(
            (
                (codes_hbm, codes_ref),
                (value_hbm, value_ref),
                (book_hbm, book_ref),
                (query_hbm, query_ref),
                (norm_hbm, norm_ref),
                (grad_hbm, grad_ref),
                (out_hbm, out_ref),
            )
        )
    ]
    for load in loads:
        load.start()

    barrier = pltpu.get_barrier_semaphore()
    pl.semaphore_signal(barrier, inc=1, device_id={"ctx": other}, device_id_type=MESH)
    over_plane(
        lambda k: pl.semaphore_signal(
            barrier, inc=1, device_id={"ctx": k * 2 + core}, device_id_type=MESH
        )
    )
    over_z(lambda k: pl.semaphore_signal(barrier, inc=1, device_id={"ch": k}, device_id_type=MESH))

    loads[0].wait()
    code_row = codes_ref[...]
    onehot[...] = jnp.where(
        lax.broadcasted_iota(jnp.int32, (codes, tokens), 0) == code_row, 1.0, 0.0
    ).astype(BF16)
    loads[1].wait()
    sums[...] = dot(onehot[...], value_ref[...])
    tally[...] = dot(jnp.ones((8, tokens), BF16), onehot[...], NT)[0:1]

    pl.semaphore_wait(barrier, 1 + (chips - 1) + (depth - 1))

    s_core = core_copy(0, sums.at[theirs], sums_x)
    s_core.start()
    t_core = core_copy(1, tally, tally_x)
    t_core.start()

    for load in loads[2:]:
        load.wait()
    norm_row = norm_ref[...]
    weight[...] = jnp.exp(dot(book_ref[...], query_ref[...], NT) * scale - norm_row)
    grads[...] = dot(weight[...].astype(BF16), grad_ref[...])
    g_core = core_copy(2, grads.at[theirs], grads_x)
    g_core.start()

    query_s[...] = query_ref[...].astype(F32)
    q_core = core_copy(7, query_s, query_x)
    n_core = core_copy(8, norm_ref, norm_x)
    q_core.start()
    n_core.start()

    s_core.wait_recv()
    sums_t[...] = sums[mine] + sums_x[...]
    far_first(lambda k: plane_copy(0, k, sums_t.at[rows(k, piece)], sums_in.at[chip]).start())
    sums_in[chip] = sums_t[rows(chip, piece)]

    g_core.wait_recv()
    grads_t[...] = grads[mine] + grads_x[...]
    grads_in[chip] = grads_t[rows(chip, piece)]

    def grads_part(n, first, size):
        def send(k):
            source = grads_t.at[pl.ds(pl.multiple_of(k * piece + first, 8), size)]
            plane_copy(n, k, source, grads_in.at[chip, pl.ds(first, size)]).start()

        far_first(send)

    t_core.wait_recv()
    tally_t[...] = tally[...] + tally_x[...]
    over_plane(lambda k: plane_copy(1, k, tally_t, tally_in.at[chip]).start())
    tally_in[chip] = tally_t[...]

    grad_s[...] = grad_ref[...].astype(F32)
    o_core = core_copy(9, grad_s, grad_x)
    o_core.start()

    key_t = dot(book_ref[...].astype(F32).T.astype(BF16), onehot[...]).astype(BF16)
    keys = key_t.astype(F32).T.astype(BF16)
    causal = lax.broadcasted_iota(jnp.int32, (tokens, tokens), 0) <= lax.broadcasted_iota(
        jnp.int32, (tokens, tokens), 1
    )
    in_block = jnp.where(
        causal, jnp.exp(dot(keys, query_ref[...], NT) * scale - norm_row), 0.0
    )
    probs[...] = in_block.astype(BF16)
    product = grad_ref[...].astype(F32) * out_ref[...].astype(F32)
    product_high, product_low = split(product)
    ones = jnp.ones((8, channels), BF16)
    delta = (dot(ones, product_high, NT) + dot(ones, product_low, NT))[0:1]
    delta_s[...] = delta
    d_core = core_copy(10, delta_s, delta_x)
    d_core.start()
    dscore = in_block * (dot(value_ref[...], grad_ref[...], NT) - delta)
    dscore_high, dscore_low = split(dscore)
    inner[...] = dot(onehot[...], dscore_high) + dot(onehot[...], dscore_low)
    i_core = core_copy(5, inner.at[theirs], inner_x)
    i_core.start()

    def plane_bytes(n, ref):
        return plane_copy(n, chip, ref, ref)

    def z_bytes(n, ref):
        return z_copy(n, z, ref, ref)

    def wait_plane(n, buffer):
        plane_bytes(n, buffer.at[pl.ds(0, chips - 1)]).wait_recv()

    def scan(buffer, result, backward):
        def step(i, total):
            k = chips - 1 - i if backward else i
            result[k] = total
            return total + buffer[k]

        lax.fori_loop(0, chips, step, jnp.zeros((piece, channels), F32))

    early_bytes = grads_t.at[pl.ds(0, (chips - 1) * early)]
    late_bytes = grads_t.at[pl.ds(0, (chips - 1) * (piece - early))]
    wait_plane(0, sums_in)
    scan(sums_in, sums_out, False)
    far_first(
        lambda k: plane_copy(3, k, sums_out.at[k], sums_p.at[rows(chip, piece)]).start()
    )
    sums_p[rows(chip, piece)] = sums_out[chip]
    if early:
        grads_part(2, 0, early)

    local_values[...] = dot(probs[...], grad_ref[...])
    lookup[0] = onehot[mine].T
    lookup[1] = onehot[theirs].T

    q_core.wait_recv()
    n_core.wait_recv()
    query_o = query_x[...].astype(BF16)
    book_half = book_ref[mine]
    weight_o[...] = jnp.exp(dot(book_half, query_o, NT) * scale - norm_x[...])
    book_half_t = book_half.astype(F32).T.astype(BF16)
    o_core.wait_recv()
    grad_o[...] = grad_x[...].astype(BF16)

    wait_plane(1, tally_in)

    def count_step(k, total):
        return total + jnp.where(k < chip, 1.0, 0.0) * tally_in[k]

    count = lax.fori_loop(0, chips, count_step, jnp.zeros((1, codes), F32))

    def half_column(row):
        column = jnp.broadcast_to(row, (128, codes)).T[:, 0:1]
        return jnp.where(core == 1, column[half:], column[:half])

    counts = half_column(count + is_one * tally_x[...])
    counts_o = half_column(count + is_zero * tally[...])
    i_core.wait_recv()
    d_core.wait_recv()

    def wait_rows(n, buffer, size):
        plane_bytes(n, buffer.at[pl.ds(0, (chips - 1) * size)]).wait_recv()

    wait_rows(3, sums_p, piece)
    if early < piece:
        grads_part(7, early, piece - early)
    cached = dot((sums_p[...] + is_zero * sums[mine]).astype(BF16), grad_o[...], NT)
    high_o, low_o = split(weight_o[...] * (cached - counts_o * delta_x[...]) + inner_x[...])
    gq_o[...] = dot(book_half_t, high_o) + dot(book_half_t, low_o)
    gq_core = core_copy(3, gq_o, gq_x)
    gq_core.start()
    cached = dot((sums_p[...] + is_one * sums_x[...]).astype(BF16), grad_ref[...], NT)
    high, low = split(weight[mine] * (cached - counts * delta) + inner[mine])
    query = query_ref[...]
    book_t[...] = (
        dot(high_o, query_o) + dot(low_o, query_o) + dot(high, query) + dot(low, query)
    ) * scale
    far_first(lambda k: plane_copy(5, k, book_t.at[rows(k, piece)], book_in.at[chip]).start())
    book_in[chip] = book_t[rows(chip, piece)]
    own = dot(book_half_t, high) + dot(book_half_t, low)
    gq_core.wait_recv()
    gq_p[...] = (own + gq_x[...]) * scale
    over_z(lambda k: z_copy(0, k, gq_p.at[rows(k, zrows)], gq_in.at[z]).start())
    gq_in[z] = gq_p[rows(z, zrows)]

    if early:
        plane_bytes(2, early_bytes).wait_recv()
    if early < piece:
        plane_bytes(7, late_bytes).wait_recv()
    scan(grads_in, grads_out, True)
    far_first(
        lambda k: plane_copy(4, k, grads_out.at[k], grads_p.at[rows(chip, piece)]).start()
    )
    grads_p[rows(chip, piece)] = grads_out[chip]

    wait_plane(5, book_in)
    book_s[...] = lax.fori_loop(
        0, chips, lambda k, total: total + book_in[k], jnp.zeros((piece, dk), F32)
    )
    over_z(lambda k: z_copy(1, k, book_s, book_z.at[z]).start())
    book_z[z] = book_s[...]

    def wait_z(n, buffer):
        z_bytes(n, buffer.at[pl.ds(0, depth - 1)]).wait_recv()

    wait_z(0, gq_in)
    gq_s[...] = lax.fori_loop(
        0, depth, lambda k, total: total + gq_in[k], jnp.zeros((zrows, tokens), F32)
    )
    over_z(lambda k: z_copy(2, k, gq_s, gq_r.at[rows(z, zrows)]).start())
    gq_r[rows(z, zrows)] = gq_s[...]

    wait_z(1, book_z)
    book_o[...] = lax.fori_loop(
        0, depth, lambda k, total: total + book_z[k], jnp.zeros((piece, dk), F32)
    )
    far_first(lambda k: plane_copy(6, k, book_o, book_r.at[rows(chip, piece)]).start())
    book_r[rows(chip, piece)] = book_o[...]

    def look_up(n, rows_later):
        later_high, later_low = split(rows_later)
        return dot(lookup[n], later_high) + dot(lookup[n], later_low)

    wait_rows(4, grads_p, piece)
    grads_f[...] = grads_p[...] + is_one * grads[mine]
    g_back = core_copy(4, grads_f, grads_h)
    g_back.start()
    local_values[...] += look_up(0, grads_p[...] + is_zero * grads_x[...])
    g_back.wait_recv()
    gv_ref[...] = (local_values[...] + look_up(1, grads_h[...])).astype(BF16)

    wait_rows(6, book_r, piece)
    b_back = core_copy(6, book_r, book_h)
    b_back.start()
    z_bytes(2, gq_r.at[pl.ds(0, (depth - 1) * zrows)]).wait_recv()
    gq_ref[...] = gq_r[...].T
    gb_ref[mine] = book_r[...]
    b_back.wait_recv()
    gb_ref[theirs] = book_h[...]

    for copy in (
        (s_core, t_core, g_core, q_core, n_core, o_core, d_core, i_core)
        + (gq_core, g_back, b_back)
    ):
        copy.wait_send()

    for n, ref in ((0, sums_in), (1, tally_in), (3, sums_out), (4, grads_out), (5, book_in)):
        plane_bytes(n, ref.at[pl.ds(0, chips - 1)]).wait_send()
    if early:
        plane_bytes(2, early_bytes).wait_send()
    if early < piece:
        plane_bytes(7, late_bytes).wait_send()
    plane_bytes(6, book_r.at[pl.ds(0, (chips - 1) * piece)]).wait_send()
    z_bytes(0, gq_in.at[pl.ds(0, depth - 1)]).wait_send()
    z_bytes(1, book_z.at[pl.ds(0, depth - 1)]).wait_send()
    z_bytes(2, gq_r.at[pl.ds(0, (depth - 1) * zrows)]).wait_send()


def store(gv_ref, gq_ref, gb_ref, gv_hbm, gq_hbm, gb_hbm, sem):
    copies = [
        pltpu.make_async_copy(source, target, sem.at[n])
        for n, (source, target) in enumerate(
            ((gv_ref, gv_hbm), (gq_ref, gq_hbm), (gb_ref, gb_hbm))
        )
    ]
    for copy in copies:
        copy.start()
    for copy in copies:
        copy.wait()


def local(chips, depth, queries, codes, codebook, values, grad_out, attn_out, normalizer):
    tokens, channels = values.shape
    count, dk = codebook.shape
    half = count // 2
    piece = half // chips
    zrows = dk // depth

    def f32(*shape):
        return pltpu.VMEM(shape, F32)

    def scan_scratch():
        return [
            f32(count, channels),
            f32(half, channels),
            f32(half, channels),
            f32(chips, piece, channels),
            f32(chips, piece, channels),
            f32(half, channels),
        ]

    scratch = (
        [
            pltpu.VMEM((1, tokens), jnp.int32),
            pltpu.VMEM((tokens, channels), BF16),
            pltpu.VMEM((count, dk), BF16),
            pltpu.VMEM((tokens, dk), BF16),
            f32(1, tokens),
            pltpu.VMEM((tokens, channels), BF16),
            pltpu.VMEM((tokens, channels), BF16),
            pltpu.SemaphoreType.DMA((7,)),
            pltpu.VMEM((count, tokens), BF16),
            f32(count, tokens),
            pltpu.VMEM((tokens, tokens), BF16),
            f32(count, tokens),
            f32(tokens, channels),
        ]
        + scan_scratch()
        + scan_scratch()
        + [f32(half, channels), f32(half, channels)]
        + [
            f32(tokens, dk),
            f32(tokens, dk),
            f32(tokens, channels),
            f32(tokens, channels),
            pltpu.VMEM((tokens, channels), BF16),
            f32(half, tokens),
            f32(half, tokens),
            f32(1, tokens),
            f32(1, tokens),
            f32(1, tokens),
            pltpu.VMEM((2, tokens, half), BF16),
        ]
        + [f32(1, count), f32(1, count), f32(1, count), f32(chips, 1, count)]
        + [
            f32(half, dk),
            f32(chips, piece, dk),
            f32(piece, dk),
            f32(depth, piece, dk),
            f32(piece, dk),
            f32(half, dk),
            f32(half, dk),
        ]
        + [f32(dk, tokens), f32(dk, tokens), f32(dk, tokens), f32(depth, zrows, tokens), f32(zrows, tokens), f32(dk, tokens)]
        + [
            pltpu.SemaphoreType.DMA((11,)),
            pltpu.SemaphoreType.DMA((11,)),
            pltpu.SemaphoreType.DMA((8,)),
            pltpu.SemaphoreType.DMA((8,)),
            pltpu.SemaphoreType.DMA((3,)),
            pltpu.SemaphoreType.DMA((3,)),
        ]
    )
    results = pl.pallas_call(
        functools.partial(kernel, chips, depth),
        out_shape=(
            pltpu.VMEM((tokens, channels), BF16),
            pltpu.VMEM((tokens, dk), F32),
            pltpu.VMEM((count, dk), F32),
        ),
        in_specs=[pl.BlockSpec(memory_space=pltpu.HBM)] * 7,
        out_specs=[pl.BlockSpec(memory_space=pltpu.VMEM)] * 3,
        scratch_shapes=scratch,
        compiler_params=pltpu.CompilerParams(
            collective_id=0, has_side_effects=True, vmem_limit_bytes=60 * 1024 * 1024
        ),
        name="vq_backward",
    )(
        codes.reshape(1, tokens),
        values,
        codebook,
        queries,
        normalizer.reshape(1, tokens),
        grad_out,
        attn_out,
    )
    return pl.pallas_call(
        store,
        out_shape=(
            jax.ShapeDtypeStruct((tokens, channels), BF16),
            jax.ShapeDtypeStruct((tokens, dk), F32),
            jax.ShapeDtypeStruct((count, dk), F32),
        ),
        in_specs=[pl.BlockSpec(memory_space=pl.ANY)] * 3,
        out_specs=[pl.BlockSpec(memory_space=pltpu.HBM)] * 3,
        scratch_shapes=[pltpu.SemaphoreType.DMA((3,))],
        compiler_params=pltpu.CompilerParams(vmem_limit_bytes=4 * 1024 * 1024),
        name="store",
    )(*results)


def solution(mesh):
    in_specs = (
        P("ctx", None),
        P("ctx"),
        P(),
        P("ctx", "ch"),
        P("ctx", "ch"),
        P("ctx", "ch"),
        P("ctx"),
    )
    out_specs = (P("ctx", "ch"), P("ctx", None), P())
    step = functools.partial(local, mesh.shape["ctx"] // 2, mesh.shape["ch"])
    return jax.shard_map(step, mesh=mesh, in_specs=in_specs, out_specs=out_specs, check_vma=False)
```

```python
import functools

import jax
import jax.numpy as jnp
from jax import lax
from jax.experimental import pallas as pl
from jax.experimental.pallas import tpu as pltpu
from jax.sharding import PartitionSpec as P

MESH = pl.DeviceIdType.MESH
F32 = jnp.float32
BF16 = jnp.bfloat16

FAR_FIRST = (
    ((2, 2), (2, 1), (1, 2), (2, 3), (3, 2), (1, 1), (1, 3), (3, 1), (3, 3), (2, 0), (0, 2))
    + ((1, 0), (3, 0), (0, 1), (0, 3))
)

NN = (((1,), (0,)), ((), ()))
NT = (((1,), (1,)), ((), ()))


def dot(a, b, dims=NN):
    return lax.dot_general(a, b, dims, preferred_element_type=F32)


def split(x):
    high = x.astype(BF16)
    return high, (x - high.astype(F32)).astype(BF16)


def kernel(
    chips,
    depth,
    codes_hbm,
    value_hbm,
    book_hbm,
    query_hbm,
    norm_hbm,
    grad_hbm,
    out_hbm,
    gv_ref,
    gq_ref,
    gb_ref,
    codes_ref,
    value_ref,
    book_ref,
    query_ref,
    norm_ref,
    grad_ref,
    out_ref,
    load_sem,
    onehot,
    weight,
    probs,
    inner,
    local_values,
    sums,
    sums_x,
    sums_t,
    sums_in,
    sums_out,
    sums_p,
    grads,
    grads_x,
    grads_t,
    grads_in,
    grads_out,
    grads_p,
    grads_f,
    grads_h,
    query_s,
    query_x,
    grad_s,
    grad_x,
    grad_o,
    weight_o,
    inner_x,
    norm_x,
    delta_s,
    delta_x,
    lookup,
    tally,
    tally_x,
    tally_t,
    tally_in,
    book_t,
    book_in,
    book_s,
    book_z,
    book_o,
    book_r,
    gq_o,
    gq_x,
    gq_p,
    gq_in,
    gq_s,
    gq_r,
    core_send,
    core_recv,
    plane_send,
    plane_recv,
    z_send,
    z_recv,
):
    tokens, channels = value_ref.shape
    codes, dk = book_ref.shape
    half = codes // 2
    piece = half // chips
    zrows = dk // depth
    quarter = half // 2
    part = piece // 2
    parts = (pl.ds(0, quarter), pl.ds(quarter, quarter))
    scale = float(dk) ** -0.5

    ctx = lax.axis_index("ctx")
    z = lax.axis_index("ch")
    chip = ctx // 2
    core = lax.rem(ctx, 2)
    other = chip * 2 + (1 - core)
    is_one = core.astype(F32)
    is_zero = 1.0 - is_one
    mine = pl.ds(pl.multiple_of(core * half, half), half)
    theirs = pl.ds(pl.multiple_of((1 - core) * half, half), half)

    def rows(k, size):
        return pl.ds(pl.multiple_of(k * size, size), size)

    def core_copy(n, src, dst):
        return pltpu.make_async_remote_copy(
            src_ref=src,
            dst_ref=dst,
            send_sem=core_send.at[n],
            recv_sem=core_recv.at[n],
            device_id={"ctx": other},
            device_id_type=MESH,
        )

    def plane_copy(n, k, src, dst):
        return pltpu.make_async_remote_copy(
            src_ref=src,
            dst_ref=dst,
            send_sem=plane_send.at[n],
            recv_sem=plane_recv.at[n],
            device_id={"ctx": k * 2 + core},
            device_id_type=MESH,
        )

    def cross_copy(k, src, dst):
        return pltpu.make_async_remote_copy(
            src_ref=src,
            dst_ref=dst,
            send_sem=plane_send.at[9],
            recv_sem=plane_recv.at[9],
            device_id={"ctx": k * 2 + (1 - core)},
            device_id_type=MESH,
        )

    def z_copy(n, k, src, dst):
        return pltpu.make_async_remote_copy(
            src_ref=src,
            dst_ref=dst,
            send_sem=z_send.at[n],
            recv_sem=z_recv.at[n],
            device_id={"ch": k},
            device_id_type=MESH,
        )

    def over_plane(body):
        def step(i, carry):
            body(lax.rem(chip + i, chips))
            return carry

        lax.fori_loop(1, chips, step, 0)

    def far_first(body):
        y, x = chip // 4, lax.rem(chip, 4)
        for dy, dx in FAR_FIRST:
            body(lax.rem(y + dy, 4) * 4 + lax.rem(x + dx, 4))

    def over_z(body):
        half_way = depth // 2
        body(lax.rem(z + half_way, depth))

        def step(i, carry):
            body(lax.rem(z + half_way + i, depth))
            body(lax.rem(z + half_way - i, depth))
            return carry

        lax.fori_loop(1, half_way, step, 0)

    loads = [
        pltpu.make_async_copy(source, target, load_sem.at[n])
        for n, (source, target) in enumerate(
            (
                (codes_hbm, codes_ref),
                (value_hbm, value_ref),
                (book_hbm, book_ref),
                (query_hbm, query_ref),
                (norm_hbm, norm_ref),
                (grad_hbm, grad_ref),
                (out_hbm, out_ref),
            )
        )
    ]
    for load in loads:
        load.start()

    barrier = pltpu.get_barrier_semaphore()
    pl.semaphore_signal(barrier, inc=1, device_id={"ctx": other}, device_id_type=MESH)

    def greet(k):
        for index in (k * 2, k * 2 + 1):
            pl.semaphore_signal(barrier, inc=1, device_id={"ctx": index}, device_id_type=MESH)

    over_plane(greet)
    over_z(lambda k: pl.semaphore_signal(barrier, inc=1, device_id={"ch": k}, device_id_type=MESH))

    loads[0].wait()
    code_row = codes_ref[...]
    onehot[...] = jnp.where(
        lax.broadcasted_iota(jnp.int32, (codes, tokens), 0) == code_row, 1.0, 0.0
    ).astype(BF16)
    loads[1].wait()
    sums[...] = dot(onehot[...], value_ref[...])
    tally[...] = dot(jnp.ones((8, tokens), BF16), onehot[...], NT)[0:1]

    pl.semaphore_wait(barrier, 1 + 2 * (chips - 1) + (depth - 1))

    s_core = core_copy(0, sums.at[theirs], sums_x)
    s_core.start()
    t_core = core_copy(1, tally, tally_x)
    t_core.start()

    for load in loads[2:]:
        load.wait()
    norm_row = norm_ref[...]
    weight[...] = jnp.exp(dot(book_ref[...], query_ref[...], NT) * scale - norm_row)
    grads[...] = dot(weight[...].astype(BF16), grad_ref[...])
    g_core = core_copy(2, grads.at[theirs], grads_x)

    query_s[...] = query_ref[...].astype(F32)
    q_core = core_copy(7, query_s, query_x)
    n_core = core_copy(8, norm_ref, norm_x)

    s_core.wait_recv()
    sums_t[...] = sums[mine] + sums_x[...]
    far_first(lambda k: plane_copy(0, k, sums_t.at[rows(k, piece)], sums_in.at[chip]).start())
    for copy in (g_core, q_core, n_core):
        copy.start()
    sums_in[chip] = sums_t[rows(chip, piece)]

    g_core.wait_recv()
    grads_t[...] = grads[mine] + grads_x[...]
    for n in (0, 1):
        grads_in[n, chip] = grads_t[pl.ds(pl.multiple_of(n * quarter + chip * part, part), part)]

    def grads_send(n):
        def send(k):
            source = grads_t.at[pl.ds(pl.multiple_of(n * quarter + k * part, part), part)]
            plane_copy((2, 7)[n], k, source, grads_in.at[n, chip]).start()

        far_first(send)

    t_core.wait_recv()
    tally_t[...] = tally[...] + tally_x[...]
    over_plane(lambda k: plane_copy(1, k, tally_t, tally_in.at[chip]).start())
    tally_in[chip] = tally_t[...]

    grad_s[...] = grad_ref[...].astype(F32)
    o_core = core_copy(9, grad_s, grad_x)
    o_core.start()

    key_t = dot(book_ref[...].astype(F32).T.astype(BF16), onehot[...]).astype(BF16)
    keys = key_t.astype(F32).T.astype(BF16)
    causal = lax.broadcasted_iota(jnp.int32, (tokens, tokens), 0) <= lax.broadcasted_iota(
        jnp.int32, (tokens, tokens), 1
    )
    in_block = jnp.where(
        causal, jnp.exp(dot(keys, query_ref[...], NT) * scale - norm_row), 0.0
    )
    probs[...] = in_block.astype(BF16)
    product = grad_ref[...].astype(F32) * out_ref[...].astype(F32)
    product_high, product_low = split(product)
    ones = jnp.ones((8, channels), BF16)
    delta = (dot(ones, product_high, NT) + dot(ones, product_low, NT))[0:1]
    delta_s[...] = delta
    d_core = core_copy(10, delta_s, delta_x)
    d_core.start()
    dscore = in_block * (dot(value_ref[...], grad_ref[...], NT) - delta)
    dscore_high, dscore_low = split(dscore)
    inner[...] = dot(onehot[...], dscore_high) + dot(onehot[...], dscore_low)
    i_core = core_copy(5, inner.at[theirs], inner_x)
    i_core.start()

    def plane_bytes(n, ref):
        return plane_copy(n, chip, ref, ref)

    def z_bytes(n, ref):
        return z_copy(n, z, ref, ref)

    def wait_plane(n, buffer):
        plane_bytes(n, buffer.at[pl.ds(0, chips - 1)]).wait_recv()

    def scan(buffer, result, backward):
        def step(i, total):
            k = chips - 1 - i if backward else i
            result[k] = total
            return total + buffer[k]

        lax.fori_loop(0, chips, step, jnp.zeros(buffer.shape[1:], F32))

    part_bytes = grads_t.at[pl.ds(0, (chips - 1) * part)]

    def grads_scan(n):
        plane_bytes((2, 7)[n], part_bytes).wait_recv()
        scan(grads_in.at[n], grads_out.at[n], True)
        place = pl.ds(pl.multiple_of(n * quarter + chip * part, part), part)
        far_first(
            lambda k: plane_copy((4, 8)[n], k, grads_out.at[n, k], grads_p.at[place]).start()
        )
        grads_p[place] = grads_out[n, chip]

    wait_plane(0, sums_in)
    scan(sums_in, sums_out, False)
    far_first(
        lambda k: plane_copy(3, k, sums_out.at[k], sums_p.at[rows(chip, piece)]).start()
    )
    sums_p[rows(chip, piece)] = sums_out[chip]
    grads_send(0)
    local_values[...] = dot(probs[...], grad_ref[...])
    lookup[0] = onehot[mine].T
    lookup[1] = onehot[theirs].T

    q_core.wait_recv()
    n_core.wait_recv()
    query_o = query_x[...].astype(BF16)
    book_half = book_ref[mine]
    weight_o[...] = jnp.exp(dot(book_half, query_o, NT) * scale - norm_x[...])
    book_half_t = book_half.astype(F32).T.astype(BF16)
    o_core.wait_recv()
    grad_o[...] = grad_x[...].astype(BF16)

    wait_plane(1, tally_in)

    def count_step(k, total):
        return total + jnp.where(k < chip, 1.0, 0.0) * tally_in[k]

    count = lax.fori_loop(0, chips, count_step, jnp.zeros((1, codes), F32))

    def half_column(row):
        column = jnp.broadcast_to(row, (128, codes)).T[:, 0:1]
        return jnp.where(core == 1, column[half:], column[:half])

    counts = half_column(count + is_one * tally_x[...])
    counts_o = half_column(count + is_zero * tally[...])
    i_core.wait_recv()
    d_core.wait_recv()

    def wait_rows(n, buffer, size):
        plane_bytes(n, buffer.at[pl.ds(0, (chips - 1) * size)]).wait_recv()

    wait_rows(3, sums_p, piece)
    grads_send(1)
    cached = dot((sums_p[...] + is_zero * sums[mine]).astype(BF16), grad_o[...], NT)
    high_o, low_o = split(weight_o[...] * (cached - counts_o * delta_x[...]) + inner_x[...])
    gq_o[...] = dot(book_half_t, high_o) + dot(book_half_t, low_o)
    gq_core = core_copy(3, gq_o, gq_x)
    gq_core.start()
    cached = dot((sums_p[...] + is_one * sums_x[...]).astype(BF16), grad_ref[...], NT)
    high, low = split(weight[mine] * (cached - counts * delta) + inner[mine])
    query = query_ref[...]
    book_t[...] = (
        dot(high_o, query_o) + dot(low_o, query_o) + dot(high, query) + dot(low, query)
    ) * scale
    far_first(lambda k: plane_copy(5, k, book_t.at[rows(k, piece)], book_in.at[chip]).start())
    book_in[chip] = book_t[rows(chip, piece)]
    own = dot(book_half_t, high) + dot(book_half_t, low)
    gq_core.wait_recv()
    gq_p[...] = (own + gq_x[...]) * scale
    over_z(lambda k: z_copy(0, k, gq_p.at[rows(k, zrows)], gq_in.at[z]).start())
    gq_in[z] = gq_p[rows(z, zrows)]

    grads_scan(0)
    grads_scan(1)

    wait_plane(5, book_in)
    book_s[...] = lax.fori_loop(
        0, chips, lambda k, total: total + book_in[k], jnp.zeros((piece, dk), F32)
    )
    over_z(lambda k: z_copy(1, k, book_s, book_z.at[z]).start())
    book_z[z] = book_s[...]

    def wait_z(n, buffer):
        z_bytes(n, buffer.at[pl.ds(0, depth - 1)]).wait_recv()

    wait_z(0, gq_in)
    gq_s[...] = lax.fori_loop(
        0, depth, lambda k, total: total + gq_in[k], jnp.zeros((zrows, tokens), F32)
    )
    over_z(lambda k: z_copy(2, k, gq_s, gq_r.at[rows(z, zrows)]).start())
    gq_r[rows(z, zrows)] = gq_s[...]

    wait_z(1, book_z)
    book_o[...] = lax.fori_loop(
        0, depth, lambda k, total: total + book_z[k], jnp.zeros((piece, dk), F32)
    )
    place = pl.ds(pl.multiple_of(core * half + chip * piece, piece), piece)

    def book_send(k):
        plane_copy(6, k, book_o, book_r.at[place]).start()
        cross_copy(k, book_o, book_r.at[place]).start()

    far_first(book_send)
    b_back = core_copy(6, book_o, book_r.at[place])
    b_back.start()
    book_r[place] = book_o[...]

    def look_up(which, n, rows_later):
        later_high, later_low = split(rows_later)
        table = lookup[which, :, parts[n]]
        return dot(table, later_high) + dot(table, later_low)

    def grads_back(n):
        plane_bytes((4, 8)[n], part_bytes).wait_recv()
        own = pl.ds(pl.multiple_of(core * half + n * quarter, quarter), quarter)
        grads_f[parts[n]] = grads_p[parts[n]] + is_one * grads[own]
        back = core_copy((4, 11)[n], grads_f.at[parts[n]], grads_h.at[parts[n]])
        back.start()
        local_values[...] += look_up(0, n, grads_p[parts[n]] + is_zero * grads_x[parts[n]])
        return back

    g_back = grads_back(0)
    g_back_late = grads_back(1)
    g_back.wait_recv()
    local_values[...] += look_up(1, 0, grads_h[parts[0]])
    g_back_late.wait_recv()
    gv_ref[...] = (local_values[...] + look_up(1, 1, grads_h[parts[1]])).astype(BF16)

    z_bytes(2, gq_r.at[pl.ds(0, (depth - 1) * zrows)]).wait_recv()
    gq_ref[...] = gq_r[...].T
    book_bytes = book_r.at[pl.ds(0, (chips - 1) * piece)]
    plane_bytes(6, book_bytes).wait_recv()
    cross_copy(chip, book_bytes, book_bytes).wait_recv()
    b_back.wait_recv()
    gb_ref[...] = book_r[...]

    for copy in (
        (s_core, t_core, g_core, q_core, n_core, o_core, d_core, i_core)
        + (gq_core, g_back, g_back_late, b_back)
    ):
        copy.wait_send()

    for n, ref in ((0, sums_in), (1, tally_in), (3, sums_out), (5, book_in)):
        plane_bytes(n, ref.at[pl.ds(0, chips - 1)]).wait_send()
    for n in (2, 7, 4, 8):
        plane_bytes(n, part_bytes).wait_send()
    plane_bytes(6, book_bytes).wait_send()
    cross_copy(chip, book_bytes, book_bytes).wait_send()
    z_bytes(0, gq_in.at[pl.ds(0, depth - 1)]).wait_send()
    z_bytes(1, book_z.at[pl.ds(0, depth - 1)]).wait_send()
    z_bytes(2, gq_r.at[pl.ds(0, (depth - 1) * zrows)]).wait_send()


def store(gv_ref, gq_ref, gb_ref, gv_hbm, gq_hbm, gb_hbm, sem):
    copies = [
        pltpu.make_async_copy(source, target, sem.at[n])
        for n, (source, target) in enumerate(
            ((gv_ref, gv_hbm), (gq_ref, gq_hbm), (gb_ref, gb_hbm))
        )
    ]
    for copy in copies:
        copy.start()
    for copy in copies:
        copy.wait()


def local(chips, depth, queries, codes, codebook, values, grad_out, attn_out, normalizer):
    tokens, channels = values.shape
    count, dk = codebook.shape
    half = count // 2
    piece = half // chips
    zrows = dk // depth

    def f32(*shape):
        return pltpu.VMEM(shape, F32)

    def scan_scratch(*cut):
        return [
            f32(count, channels),
            f32(half, channels),
            f32(half, channels),
            f32(*cut, channels),
            f32(*cut, channels),
            f32(half, channels),
        ]

    scratch = (
        [
            pltpu.VMEM((1, tokens), jnp.int32),
            pltpu.VMEM((tokens, channels), BF16),
            pltpu.VMEM((count, dk), BF16),
            pltpu.VMEM((tokens, dk), BF16),
            f32(1, tokens),
            pltpu.VMEM((tokens, channels), BF16),
            pltpu.VMEM((tokens, channels), BF16),
            pltpu.SemaphoreType.DMA((7,)),
            pltpu.VMEM((count, tokens), BF16),
            f32(count, tokens),
            pltpu.VMEM((tokens, tokens), BF16),
            f32(count, tokens),
            f32(tokens, channels),
        ]
        + scan_scratch(chips, piece)
        + scan_scratch(2, chips, piece // 2)
        + [f32(half, channels), f32(half, channels)]
        + [
            f32(tokens, dk),
            f32(tokens, dk),
            f32(tokens, channels),
            f32(tokens, channels),
            pltpu.VMEM((tokens, channels), BF16),
            f32(half, tokens),
            f32(half, tokens),
            f32(1, tokens),
            f32(1, tokens),
            f32(1, tokens),
            pltpu.VMEM((2, tokens, half), BF16),
        ]
        + [f32(1, count), f32(1, count), f32(1, count), f32(chips, 1, count)]
        + [
            f32(half, dk),
            f32(chips, piece, dk),
            f32(piece, dk),
            f32(depth, piece, dk),
            f32(piece, dk),
            f32(count, dk),
        ]
        + [f32(dk, tokens), f32(dk, tokens), f32(dk, tokens), f32(depth, zrows, tokens), f32(zrows, tokens), f32(dk, tokens)]
        + [
            pltpu.SemaphoreType.DMA((12,)),
            pltpu.SemaphoreType.DMA((12,)),
            pltpu.SemaphoreType.DMA((10,)),
            pltpu.SemaphoreType.DMA((10,)),
            pltpu.SemaphoreType.DMA((3,)),
            pltpu.SemaphoreType.DMA((3,)),
        ]
    )
    results = pl.pallas_call(
        functools.partial(kernel, chips, depth),
        out_shape=(
            pltpu.VMEM((tokens, channels), BF16),
            pltpu.VMEM((tokens, dk), F32),
            pltpu.VMEM((count, dk), F32),
        ),
        in_specs=[pl.BlockSpec(memory_space=pltpu.HBM)] * 7,
        out_specs=[pl.BlockSpec(memory_space=pltpu.VMEM)] * 3,
        scratch_shapes=scratch,
        compiler_params=pltpu.CompilerParams(
            collective_id=0, has_side_effects=True, vmem_limit_bytes=60 * 1024 * 1024
        ),
        name="vq_backward",
    )(
        codes.reshape(1, tokens),
        values,
        codebook,
        queries,
        normalizer.reshape(1, tokens),
        grad_out,
        attn_out,
    )
    return pl.pallas_call(
        store,
        out_shape=(
            jax.ShapeDtypeStruct((tokens, channels), BF16),
            jax.ShapeDtypeStruct((tokens, dk), F32),
            jax.ShapeDtypeStruct((count, dk), F32),
        ),
        in_specs=[pl.BlockSpec(memory_space=pl.ANY)] * 3,
        out_specs=[pl.BlockSpec(memory_space=pltpu.HBM)] * 3,
        scratch_shapes=[pltpu.SemaphoreType.DMA((3,))],
        compiler_params=pltpu.CompilerParams(vmem_limit_bytes=4 * 1024 * 1024),
        name="store",
    )(*results)


def solution(mesh):
    in_specs = (
        P("ctx", None),
        P("ctx"),
        P(),
        P("ctx", "ch"),
        P("ctx", "ch"),
        P("ctx", "ch"),
        P("ctx"),
    )
    out_specs = (P("ctx", "ch"), P("ctx", None), P())
    step = functools.partial(local, mesh.shape["ctx"] // 2, mesh.shape["ch"])
    return jax.shard_map(step, mesh=mesh, in_specs=in_specs, out_specs=out_specs, check_vma=False)
```
